32 devices in a mesh: parts: 2 (over y), row: 4 (over x, core), col: 4 (over z).
Axes of the slice: x: 2, y: 2, z: 4, core: 2. Of those that a mesh axis runs over, the one named last changes fastest.
Arguments:
- atom_feats: bfloat16 [2048, 128], P(('parts', 'row', 'col')), parts along dimension 0, may hold values from -6 to 6
- atom_bias: bfloat16 [4, 2048, 128], P(None, ('parts', 'row', 'col')), parts along dimension 1, may hold values from -6 to 300
- key_mask: int32 [64, 128], P(('parts', 'row', 'col')), parts along dimension 0, may hold values 0 or 1
- atom_token: int32 [2048], P('parts'), parts along dimension 0, may hold values from 0 to 191, never falling along the last dimension, each value on 1 to 10 neighbouring positions
- token_mask: int32 [384], P('parts'), parts along dimension 0, may hold values 0 or 1
- pair: bfloat16 [384, 192, 128], P(('parts', 'row'), 'col'), parts along dimension 0, may hold values from -6 to 6
- atom_norms: float32 [3, 2, 128], replicated, may hold values from 0.25 to 1.75
- w_atom_qkv: bfloat16 [3, 128, 384], replicated, may hold values from -0.5 to 0.5
- w_atom_gate: bfloat16 [3, 128, 128], replicated, may hold values from -0.5 to 0.5
- w_atom_out: bfloat16 [3, 128, 128], replicated, may hold values from -0.5 to 0.5
- w_atom_up: bfloat16 [3, 128, 512], replicated, may hold values from -0.5 to 0.5
- w_atom_down: bfloat16 [3, 256, 128], replicated, may hold values from -0.375 to 0.375
- w_agg: bfloat16 [128, 768], replicated, may hold values from -0.5 to 0.5
- token_norm: float32 [768], replicated, may hold values from 0.25 to 1.75
- w_token: bfloat16 [4, 768, 384], replicated, may hold values from -0.21875 to 0.21875
- pair_norms: float32 [3, 128], replicated, may hold values from 0.25 to 1.75
- w_pair_up: bfloat16 [2, 128, 1024], replicated, may hold values from -0.5 to 0.5
- w_pair_down: bfloat16 [2, 512, 128], replicated, may hold values from -0.25 to 0.25
- w_bias: float32 [128, 8], replicated, may hold values from -16 to 16
Outputs:
- atom_out: bfloat16 [2048, 128], P(('parts', 'row', 'col')), parts along dimension 0
- token_out: bfloat16 [384, 384], P(('parts', 'row')), parts along dimension 0
The draws below stay inside these ranges and needn't reach their ends.
There are 2 independent parts, one for each index of `parts`. The reference program is written for one: setup_inputs(seed, part) draws one part's arguments, and reference() takes and returns one part's arrays. A program takes and returns all parts, laid end to end along the dimension named above; an argument that names none is the same for every part. Nothing has to cross between parts.
Inputs may be any that keep to these rules, and one draw needn't show every extreme that they name: `atom_token`: token numbers never fall along the atoms; every token has 1 to 10 atoms and some token has exactly 10.
All inputs are finite; a program needn't handle non-finite values. No bound on the sum of `key_mask` on one device may be relied on, other than what follows from the above.
Results may differ from the reference program's by a relative error of at most 0.024.
The reference program's roundings to bfloat16 on the way count: a program that leaves them out, or rounds other values in their place, can miss the bound.
Values may be sent and summed in bfloat16 or wider, within the bound.
A program may use at most 64 MiB of HBM per device.

```python
import math
import jax
import jax.numpy as jnp
import numpy as np
from jax import lax

C_ATOM = 128
ATOM_HEADS = 4
ATOM_FF = 256
ATOM_BLOCKS = 3
QWIN = 32
KWIN = 128
N_ATOMS = 1024
C_TOKEN = 768
HEADS = 8
HEAD = 48
HD = 384
C_PAIR = 128
PAIR_FF = 512
TRANS = 2
NTOK = 192
MOST_ATOMS = 10
N_ROW = 4


def draw_atom_bias(key, part):
    shape = (ATOM_HEADS, N_ATOMS, KWIN)
    keys = jax.random.split(jax.random.fold_in(key, 11), 1)
    base = jax.random.normal(keys[0], shape, jnp.float32)
    return jnp.clip(base, -6.0, 300.0).astype(jnp.bfloat16)


def draw_w_bias(key, part):
    shape = (C_PAIR, HEADS)
    base = jax.random.normal(jax.random.fold_in(key, 23), shape, jnp.float32)
    return jnp.clip(base * C_PAIR ** (-0.5), -16.0, 16.0)


def set_ends(result, rng, least, largest):
    dims = result.shape
    place = [jax.random.randint(jax.random.fold_in(rng, axis), (), 0, dims[axis]) for axis in range(len(dims))]
    result = result.at[tuple(place)].set(least)
    longest = dims.index(max(dims))
    place[longest] = (place[longest] + 1) % dims[longest]
    return result.at[tuple(place)].set(largest)


def level_of(own_key, shape, pieces, smallest, top_value):
    def one(position, blocks):
        draws = jax.random.uniform(jax.random.fold_in(jax.random.fold_in(own_key, 6), position), (blocks,), jnp.float32, smallest / len(pieces), top_value / len(pieces))
        return jnp.repeat(jnp.exp(draws), shape[position] // blocks).reshape((-1,) + (1,) * (len(shape) - position - 1))

    level = one(*pieces[0])
    for cut in pieces[1:]:
        level = level * one(*cut)
    return level


def split_up(number_of, total, limit, slope):
    portions = [(1 << 20) // math.isqrt(rank ** slope) + 1 for rank in range(2, number_of + 1)]
    spare, given = total - limit - (number_of - 1), [1] * (number_of - 1)
    while spare > 0:
        free = [i for i in range(number_of - 1) if given[i] < limit]
        pool, budget = sum([portions[i] for i in free]), spare
        for i in free:
            addition = min(limit - given[i], max(1, budget * portions[i] // pool), spare)
            given[i] = given[i] + addition
            spare = spare - addition
    return np.array([limit] + given)


def uneven(key, amount, total, reach, lean):
    if amount == 2:
        one = jax.random.randint(key, (), max(1, total - reach), min(reach, total - 1) + 1)
        return jnp.stack([one, total - one])
    tallies = jnp.asarray(split_up(amount, total, reach, lean), jnp.int32)
    pairs = (amount - 1) // 2
    donor, sink = tallies[1:1 + 2 * pairs:2], tallies[2:2 + 2 * pairs:2]
    slack = jnp.minimum(donor - 1, reach - sink)
    shifted = jax.random.randint(jax.random.fold_in(key, 1), (pairs,), 0, 1 << 20) % (slack + 1)
    tallies = tallies.at[1:1 + 2 * pairs:2].set(donor - shifted).at[2:2 + 2 * pairs:2].set(sink + shifted)
    return tallies[jax.random.permutation(jax.random.fold_in(key, 2), amount)]


def gaussian(stream_key, dims, scale, most, shards=(), kind=jnp.bfloat16):
    entries = scale * jax.random.normal(stream_key, dims, jnp.float32)
    if shards:
        entries = entries * level_of(stream_key, dims, shards, -0.22, 0.18)
    return jnp.clip(entries, -most, most).astype(kind)


def setup_inputs(seed: int = 0, part: int = 0) -> dict:
    key_list = jax.random.split(jax.random.key(seed), 20)
    part_keys = jax.random.split(jax.random.fold_in(key_list[19], part), 20)
    atom_feats = gaussian(part_keys[0], (N_ATOMS, C_ATOM), 1.0, 6.0, ((0, 16),))
    atom_bias = draw_atom_bias(jax.random.fold_in(jax.random.fold_in(key_list[19], part), 71), part)
    key_mask = set_ends((jax.random.randint(part_keys[2], (N_ATOMS // QWIN, KWIN), 0, 4) < 3).astype(jnp.int32), jax.random.fold_in(part_keys[2], 1), 0, 1)
    atom_token = jnp.searchsorted(jnp.cumsum(uneven(part_keys[3], NTOK, N_ATOMS, MOST_ATOMS, 2)), jnp.arange(N_ATOMS), side="right").astype(jnp.int32)
    token_mask = set_ends((jax.random.randint(part_keys[4], (NTOK,), 0, 8) < 7).astype(jnp.int32), jax.random.fold_in(part_keys[4], 1), 0, 1)
    pair = gaussian(part_keys[5], (NTOK, NTOK, C_PAIR), 1.0, 6.0, ((0, 4), (1, 4)))
    atom_norms = jnp.clip(1.0 + 0.15 * jax.random.normal(key_list[6], (ATOM_BLOCKS, 2, C_ATOM), jnp.float32), 0.25, 1.75)
    w_atom_qkv = gaussian(key_list[7], (ATOM_BLOCKS, C_ATOM, 3 * C_ATOM), C_ATOM ** -0.5, 0.5)
    w_atom_gate = gaussian(key_list[8], (ATOM_BLOCKS, C_ATOM, C_ATOM), C_ATOM ** -0.5, 0.5)
    w_atom_out = gaussian(key_list[9], (ATOM_BLOCKS, C_ATOM, C_ATOM), C_ATOM ** -0.5, 0.5)
    w_atom_up = gaussian(key_list[10], (ATOM_BLOCKS, C_ATOM, 2 * ATOM_FF), C_ATOM ** -0.5, 0.5)
    w_atom_down = gaussian(key_list[11], (ATOM_BLOCKS, ATOM_FF, C_ATOM), ATOM_FF ** -0.5, 0.375)
    w_agg = gaussian(key_list[12], (C_ATOM, C_TOKEN), C_ATOM ** -0.5, 0.5)
    token_norm = jnp.clip(1.0 + 0.15 * jax.random.normal(key_list[13], (C_TOKEN,), jnp.float32), 0.25, 1.75)
    w_token = gaussian(key_list[14], (4, C_TOKEN, HD), C_TOKEN ** -0.5, 0.21875)
    pair_norms = jnp.clip(1.0 + 0.15 * jax.random.normal(key_list[15], (TRANS + 1, C_PAIR), jnp.float32), 0.25, 1.75)
    w_pair_up = gaussian(key_list[16], (TRANS, C_PAIR, 2 * PAIR_FF), C_PAIR ** -0.5, 0.5)
    w_pair_down = gaussian(key_list[17], (TRANS, PAIR_FF, C_PAIR), PAIR_FF ** -0.5, 0.25)
    w_bias = draw_w_bias(jax.random.fold_in(key_list[19], 71), part)
    return {"atom_feats": atom_feats, "atom_bias": atom_bias, "key_mask": key_mask, "atom_token": atom_token, "token_mask": token_mask, "pair": pair, "atom_norms": atom_norms, "w_atom_qkv": w_atom_qkv, "w_atom_gate": w_atom_gate, "w_atom_out": w_atom_out, "w_atom_up": w_atom_up, "w_atom_down": w_atom_down, "w_agg": w_agg, "token_norm": token_norm, "w_token": w_token, "pair_norms": pair_norms, "w_pair_up": w_pair_up, "w_pair_down": w_pair_down, "w_bias": w_bias}


EPSILON = 1e-05
NEGATIVE = -1e+30

def layer_norm(inputs, gain):
    inputs = inputs.astype(jnp.float32)
    average = lax.optimization_barrier(jnp.mean(inputs, axis=-1, keepdims=True))
    centered = inputs - average
    variance = lax.optimization_barrier(jnp.mean(centered * centered, axis=-1, keepdims=True))
    return centered * lax.rsqrt(variance + EPSILON) * gain

def swiglu(normed, w_up, w_down):
    both_parts = jnp.dot(normed, w_up, preferred_element_type=jnp.float32)
    half_width = both_parts.shape[-1] // 2
    hidden = (jax.nn.silu(both_parts[..., :half_width]) * both_parts[..., half_width:]).astype(jnp.bfloat16)
    return jnp.dot(hidden, w_down, preferred_element_type=jnp.float32)

def atom_block(state, atom_bias, usable, norms, w_qkv, w_gate, w_out, w_up, w_down):
    n_atoms, width = state.shape
    head_size = width // ATOM_HEADS
    margin = (KWIN - QWIN) // 2
    normed = layer_norm(state, norms[0]).astype(jnp.bfloat16)
    qkv = jnp.dot(normed, w_qkv, preferred_element_type=jnp.float32)
    queries = qkv[:, :width].astype(jnp.bfloat16)
    keyvals = qkv[:, width:].astype(jnp.bfloat16)
    padded = jnp.pad(keyvals, ((margin, margin), (0, 0)))
    n_win = n_atoms // QWIN
    window_rows = jnp.arange(n_win, dtype=jnp.int32)[:, None] * QWIN + jnp.arange(KWIN, dtype=jnp.int32)[None, :]
    windows = padded[window_rows]
    key_rows = windows[..., :width].reshape(n_win, KWIN, ATOM_HEADS, head_size).astype(jnp.float32)
    val_rows = windows[..., width:].reshape(n_win, KWIN, ATOM_HEADS, head_size).astype(jnp.float32)
    query_rows = queries.reshape(n_win, QWIN, ATOM_HEADS, head_size).astype(jnp.float32)
    scores = jnp.einsum('wqhd,wkhd->whqk', query_rows, key_rows) / jnp.sqrt(jnp.float32(head_size))
    bias_rows = atom_bias.astype(jnp.float32).reshape(ATOM_HEADS, n_win, QWIN, KWIN).transpose(1, 0, 2, 3)
    scores = scores + bias_rows
    mask_rows = usable[:, None, None, :]
    scores = jnp.where(mask_rows, scores, NEGATIVE)
    row_top = lax.optimization_barrier(jnp.max(scores, axis=-1, keepdims=True))
    weights = jnp.where(mask_rows, jnp.exp(scores - row_top), 0.0)
    totals = lax.optimization_barrier(jnp.sum(weights, axis=-1))
    weighted = jnp.einsum('whqk,wkhd->wqhd', weights.astype(jnp.bfloat16).astype(jnp.float32), val_rows)
    attended = (weighted / totals.transpose(0, 2, 1)[..., None]).reshape(n_atoms, width)
    gate_rows = jax.nn.sigmoid(jnp.dot(normed, w_gate, preferred_element_type=jnp.float32))
    mixed = (gate_rows * attended).astype(jnp.bfloat16)
    state = state + jnp.dot(mixed, w_out, preferred_element_type=jnp.float32)
    normed_two = layer_norm(state, norms[1]).astype(jnp.bfloat16)
    return state + swiglu(normed_two, w_up, w_down)

def reference(atom_feats, atom_bias, key_mask, atom_token, token_mask, pair, atom_norms, w_atom_qkv, w_atom_gate, w_atom_out, w_atom_up, w_atom_down, w_agg, token_norm, w_token, pair_norms, w_pair_up, w_pair_down, w_bias):
    n_atoms = atom_feats.shape[0]
    margin = (KWIN - QWIN) // 2
    n_win = n_atoms // QWIN
    key_slot = jnp.arange(KWIN, dtype=jnp.int32)
    key_index = jnp.arange(n_win, dtype=jnp.int32)[:, None] * QWIN - margin + key_slot[None, :]
    own_window = (key_slot >= margin) & (key_slot < margin + QWIN)
    usable = (key_index >= 0) & (key_index < n_atoms) & (key_mask == 1) | own_window[None, :]
    state = atom_feats.astype(jnp.float32)
    for block_number in range(ATOM_BLOCKS):
        state = atom_block(state, atom_bias, usable, atom_norms[block_number], w_atom_qkv[block_number], w_atom_gate[block_number], w_atom_out[block_number], w_atom_up[block_number], w_atom_down[block_number])
    atom_out = state.astype(jnp.bfloat16)
    feat = jax.nn.relu(jnp.dot(atom_out, w_agg, preferred_element_type=jnp.float32)).astype(jnp.bfloat16)
    sums = jax.ops.segment_sum(feat.astype(jnp.float32), atom_token, num_segments=NTOK)
    counts = jax.ops.segment_sum(jnp.ones((n_atoms,), jnp.float32), atom_token, num_segments=NTOK)
    token_normed = layer_norm(sums / counts[:, None], token_norm).astype(jnp.bfloat16)
    projected = [jnp.dot(token_normed, w_token[which], preferred_element_type=jnp.float32).astype(jnp.bfloat16) for which in range(4)]

    def pair_rows(rows):
        state_z = rows.astype(jnp.float32)
        for which in range(TRANS):
            normed = layer_norm(state_z, pair_norms[which]).astype(jnp.bfloat16)
            state_z = state_z + swiglu(normed, w_pair_up[which], w_pair_down[which])
        final_norm = layer_norm(state_z, pair_norms[TRANS])
        return jnp.einsum('ijc,ch->hij', final_norm, w_bias, precision=lax.Precision.HIGHEST)
    blocks = lax.map(pair_rows, pair.reshape(N_ROW, NTOK // N_ROW, NTOK, pair.shape[2]))
    pair_bias = blocks.transpose(1, 0, 2, 3).reshape(HEADS, NTOK, NTOK)
    queries = projected[0].reshape(NTOK, HEADS, HEAD).astype(jnp.float32)
    key_rows = projected[1].reshape(NTOK, HEADS, HEAD).astype(jnp.float32)
    val_rows = projected[2].reshape(NTOK, HEADS, HEAD).astype(jnp.float32)
    scores = jnp.einsum('ihd,jhd->hij', queries, key_rows) / jnp.sqrt(jnp.float32(HEAD)) + pair_bias
    token_index = jnp.arange(NTOK, dtype=jnp.int32)
    allowed = (token_mask[None, :] == 1) | (token_index[:, None] == token_index[None, :])
    scores = jnp.where(allowed[None], scores, NEGATIVE)
    row_top = lax.optimization_barrier(jnp.max(scores, axis=-1, keepdims=True))
    weights = jnp.where(allowed[None], jnp.exp(scores - row_top), 0.0)
    totals = lax.optimization_barrier(jnp.sum(weights, axis=-1))
    weighted = jnp.einsum('hij,jhd->ihd', weights.astype(jnp.bfloat16).astype(jnp.float32), val_rows)
    attended = weighted / totals.T[:, :, None]
    gate_rows = jax.nn.sigmoid(projected[3].astype(jnp.float32)).reshape(NTOK, HEADS, HEAD)
    token_out = (gate_rows * attended).reshape(NTOK, HEADS * HEAD).astype(jnp.bfloat16)
    return (atom_out, token_out)
```

```python
import functools

import jax
import jax.numpy as jnp
from jax import lax
from jax.experimental import pallas as pl
from jax.experimental.pallas import tpu as pltpu
from jax.sharding import PartitionSpec as P

ATOM_HEADS = 4
ATOM_BLOCKS = 3
QWIN = 32
KWIN = 128
TRANS = 2
PAIR_ROWS = 8
ATOM_STEP = 1024

EPSILON = 1e-05
NEGATIVE = -1e30
F32 = jnp.float32
BF16 = jnp.bfloat16
MESH = pl.DeviceIdType.MESH


def layer_norm(inputs, gain):
    average = jnp.mean(inputs, axis=-1, keepdims=True)
    centered = inputs - average
    variance = jnp.mean(centered * centered, axis=-1, keepdims=True)
    return centered * lax.rsqrt(variance + EPSILON) * gain


def sigmoid(value):
    return 0.5 * jnp.tanh(0.5 * value) + 0.5


def mm(left, right):
    return jnp.dot(left, right, preferred_element_type=F32)


def mm_nt(left, right):
    return lax.dot_general(left, right, (((1,), (1,)), ((), ())), preferred_element_type=F32)


def swiglu(normed, w_up, w_down):
    half = w_up.shape[1] // 2
    first = mm(normed, w_up[:, :half])
    second = mm(normed, w_up[:, half:])
    hidden = (first * sigmoid(first) * second).astype(BF16)
    return mm(hidden, w_down)


def split(value):
    high = value.astype(BF16)
    rest = value - high.astype(F32)
    middle = rest.astype(BF16)
    low = (rest - middle.astype(F32)).astype(BF16)
    return high, middle, low


def kernel(
    n_row,
    n_col,
    feats_ref,
    key_mask_ref,
    atom_token_ref,
    token_mask_ref,
    atom_norms_ref,
    token_norm_ref,
    pair_norms_ref,
    w_bias_ref,
    bias_any,
    qkv_any,
    gate_any,
    out_any,
    up_any,
    down_any,
    pair_any,
    pair_up_any,
    pair_down_any,
    agg_any,
    token_any,
    atom_out_ref,
    token_out_ref,
    bias_ref,
    qkv_ref,
    gate_ref,
    out_ref,
    up_ref,
    down_ref,
    pair_ref,
    pair_up_ref,
    pair_down_ref,
    agg_ref,
    token_ref,
    normed_buf,
    rim_buf,
    gathered,
    pair_bias_buf,
    bias_full,
    sums_ref,
    counts_ref,
    token_normed_ref,
    load_sem,
    halo_send,
    halo_recv,
    col_send,
    col_recv,
    row_send,
    row_recv,
    bias_send,
    bias_recv,
):
    row, col = lax.axis_index("row"), lax.axis_index("col")
    rank = row * n_col + col
    n_rank = n_row * n_col
    after, before = lax.rem(rank + 1, n_rank), lax.rem(rank + n_rank - 1, n_rank)
    after_id = {"row": after // n_col, "col": lax.rem(after, n_col)}
    before_id = {"row": before // n_col, "col": lax.rem(before, n_col)}
    col_peers = [lax.rem(col + d, n_col) for d in range(1, n_col)]
    row_peers = [lax.rem(row + d, n_row) for d in range(1, n_row)]

    barrier = pltpu.get_barrier_semaphore()
    for peer in [after_id, before_id] + [{"col": c} for c in col_peers] + [
        {"row": r} for r in row_peers
    ]:
        pl.semaphore_signal(barrier, inc=1, device_id=peer, device_id_type=MESH)

    loads = [
        pltpu.make_async_copy(source, target, load_sem.at[k])
        for k, (source, target) in enumerate(
            (
                (qkv_any, qkv_ref),
                (gate_any, gate_ref),
                (pair_any, pair_ref),
                (pair_up_any, pair_up_ref),
                (pair_down_any, pair_down_ref),
                (bias_any, bias_ref),
                (out_any, out_ref),
                (up_any, up_ref),
                (down_any, down_ref),
                (agg_any, agg_ref),
                (token_any, token_ref),
            )
        )
    ]
    for load in loads:
        load.start()

    atom_rows, width = feats_ref.shape
    head_size = width // ATOM_HEADS
    margin = (KWIN - QWIN) // 2
    n_win = atom_rows // QWIN
    tile = pair_ref.shape[0]
    heads = w_bias_ref.shape[1]
    n_tok = token_mask_ref.shape[1]
    n_chunk = tile // PAIR_ROWS
    flat = PAIR_ROWS * tile

    slot = lax.broadcasted_iota(jnp.int32, (1, KWIN), 1)
    own_window = (slot >= margin) & (slot < margin + QWIN)
    usable = []
    for win in range(n_win):
        key_index = rank * atom_rows + win * QWIN - margin + slot
        inside = (key_index >= 0) & (key_index < n_rank * atom_rows)
        live = (key_mask_ref[win : win + 1, :] == 1) & inside | own_window
        usable.append(jnp.where(live, 0.0, NEGATIVE))

    lane = lax.broadcasted_iota(jnp.int32, (ATOM_HEADS * QWIN, width), 1)
    line = lax.broadcasted_iota(jnp.int32, (ATOM_HEADS * QWIN, width), 0)
    head_lanes = (lane // head_size) == (line // QWIN)

    w_bias_t = w_bias_ref[...].T
    wb_high, wb_middle, wb_low = split(w_bias_t)
    none = jnp.zeros(wb_low.shape, F32)
    wb_stack = jnp.concatenate(
        [
            jnp.concatenate([wb_high.astype(F32), wb_high.astype(F32)], axis=1),
            jnp.concatenate([wb_middle.astype(F32), wb_middle.astype(F32)], axis=1),
            jnp.concatenate([wb_low.astype(F32), none], axis=1),
            jnp.zeros((heads, 2 * width), F32),
        ],
        axis=0,
    ).astype(BF16)

    def bias_copies(chunk):
        return [
            pltpu.make_async_remote_copy(
                src_ref=pair_bias_buf.at[chunk, col],
                dst_ref=pair_bias_buf.at[chunk, col],
                send_sem=bias_send.at[chunk, d],
                recv_sem=bias_recv.at[chunk, d],
                device_id={"col": peer},
                device_id_type=MESH,
            )
            for d, peer in enumerate(col_peers)
        ]

    def pair_chunk(chunk):
        z = pair_ref[pl.ds(chunk * PAIR_ROWS, PAIR_ROWS)].astype(F32).reshape(flat, width)
        for which in range(TRANS):
            normed = layer_norm(z, pair_norms_ref[which : which + 1, :]).astype(BF16)
            z = z + swiglu(normed, pair_up_ref[which], pair_down_ref[which])
        final = layer_norm(z, pair_norms_ref[TRANS : TRANS + 1, :])
        high, middle, low = split(final)
        stacked = mm_nt(wb_stack, jnp.concatenate([high, middle], axis=1))
        total = mm_nt(wb_high, low) + stacked[2 * heads : 3 * heads]
        total = total + stacked[heads : 2 * heads] + stacked[:heads]
        pair_bias_buf[chunk, col] = total
        for copy in bias_copies(chunk):
            copy.start()

    def arrange(chunk):
        for copy in bias_copies(chunk):
            copy.wait()
        for i in range(PAIR_ROWS):
            bias_full[chunk * PAIR_ROWS + i] = jnp.concatenate(
                [pair_bias_buf[chunk, c, :, i * tile : (i + 1) * tile] for c in range(n_col)],
                axis=1,
            )

    def atom_block(block, state):
        normed = layer_norm(state, atom_norms_ref[block, 0:1, :]).astype(BF16)
        normed_buf[block] = normed
        forward = pltpu.make_async_remote_copy(
            src_ref=normed_buf.at[block, pl.ds(atom_rows - margin, margin)],
            dst_ref=rim_buf.at[block, 0],
            send_sem=halo_send.at[block, 0],
            recv_sem=halo_recv.at[block, 0],
            device_id=after_id,
            device_id_type=MESH,
        )
        backward = pltpu.make_async_remote_copy(
            src_ref=normed_buf.at[block, pl.ds(0, margin)],
            dst_ref=rim_buf.at[block, 1],
            send_sem=halo_send.at[block, 1],
            recv_sem=halo_recv.at[block, 1],
            device_id=before_id,
            device_id_type=MESH,
        )
        forward.start()
        backward.start()
        w_qkv = qkv_ref[block]
        qkv = mm(normed, w_qkv)
        gate_rows = sigmoid(mm(normed, gate_ref[block]))
        pair_chunk(block)
        forward.wait()
        backward.wait()
        w_kv = w_qkv[:, width:]
        rim = rim_buf[block].reshape(2 * margin, width)
        rim_kv = mm(rim, w_kv).astype(BF16)
        keyvals = jnp.concatenate(
            [rim_kv[:margin], qkv[:, width:].astype(BF16), rim_kv[margin:]], axis=0
        )
        attended = []
        for win in range(n_win):
            rows = slice(win * QWIN, (win + 1) * QWIN)
            query = jnp.concatenate([qkv[rows, :width]] * ATOM_HEADS, axis=0)
            query = jnp.where(head_lanes, query, 0.0).astype(BF16)
            window = keyvals[win * QWIN : win * QWIN + KWIN]
            bias = bias_ref[:, rows, :].astype(F32).reshape(ATOM_HEADS * QWIN, KWIN)
            scores = mm_nt(query, window[:, :width]) * (head_size**-0.5) + bias
            scores = jnp.where(usable[win] == 0.0, scores, NEGATIVE)
            weights = jnp.exp(scores - jnp.max(scores, axis=-1, keepdims=True))
            totals = jnp.sum(weights, axis=-1, keepdims=True)
            weighted = mm(weights.astype(BF16), window[:, width:]) / totals
            weighted = jnp.where(head_lanes, weighted, 0.0)
            attended.append(
                sum(weighted[h * QWIN : (h + 1) * QWIN] for h in range(ATOM_HEADS))
            )
        mixed = (gate_rows * jnp.concatenate(attended, axis=0)).astype(BF16)
        state = state + mm(mixed, out_ref[block])
        normed_two = layer_norm(state, atom_norms_ref[block, 1:2, :]).astype(BF16)
        return state + swiglu(normed_two, up_ref[block], down_ref[block])

    pl.semaphore_wait(barrier, 2 + n_col - 1 + n_row - 1)
    for load in loads[:9]:
        load.wait()
    state = lax.fori_loop(0, ATOM_BLOCKS, atom_block, feats_ref[...].astype(F32))
    atom_out = state.astype(BF16)
    atom_out_ref[...] = atom_out
    gathered[row, col] = atom_out

    along_col = [
        pltpu.make_async_remote_copy(
            src_ref=gathered.at[row, col],
            dst_ref=gathered.at[row, col],
            send_sem=col_send.at[d],
            recv_sem=col_recv.at[d],
            device_id={"col": peer},
            device_id_type=MESH,
        )
        for d, peer in enumerate(col_peers)
    ]
    for copy in along_col:
        copy.start()
    pair_chunk(ATOM_BLOCKS)
    for copy in along_col:
        copy.wait()
    along_row = [
        pltpu.make_async_remote_copy(
            src_ref=gathered.at[row],
            dst_ref=gathered.at[row],
            send_sem=row_send.at[d],
            recv_sem=row_recv.at[d],
            device_id={"row": peer},
            device_id_type=MESH,
        )
        for d, peer in enumerate(row_peers)
    ]
    for copy in along_row:
        copy.start()

    def rest(chunk, carry):
        pair_chunk(chunk)
        return carry

    lax.fori_loop(ATOM_BLOCKS + 1, n_chunk, rest, 0)

    def place(chunk, carry):
        arrange(chunk)
        return carry

    lax.fori_loop(0, n_chunk - 1, place, 0)
    for load in loads[9:]:
        load.wait()
    for copy in along_row:
        copy.wait()

    step_rows = max(1, min(n_row, ATOM_STEP // (n_col * atom_rows)))
    step_atoms = step_rows * n_col * atom_rows
    steps = n_row // step_rows
    w_agg = agg_ref[...]
    token_at = lax.broadcasted_iota(jnp.int32, (n_tok, step_atoms), 0)

    def partial_sums(step):
        atoms = gathered[pl.ds(step * step_rows, step_rows)].reshape(step_atoms, width)
        feat = jnp.maximum(mm(atoms, w_agg), 0.0).astype(BF16)
        tokens = atom_token_ref[:, pl.ds(pl.multiple_of(step * step_atoms, 128), step_atoms)]
        onehot = jnp.where(token_at == tokens, 1.0, 0.0)
        return mm(onehot.astype(BF16), feat), jnp.sum(onehot, axis=1, keepdims=True)

    sums, counts = partial_sums(0)
    if steps > 1:
        sums_ref[...] = sums
        counts_ref[...] = counts

        def more(step, carry):
            extra, number = partial_sums(step)
            sums_ref[...] += extra
            counts_ref[...] += number
            return carry

        lax.fori_loop(1, steps, more, 0)
        sums = sums_ref[...]
        counts = counts_ref[...]
    token_normed = layer_norm(sums / counts, token_norm_ref[...]).astype(BF16)
    token_normed_ref[...] = token_normed
    keys = mm(token_normed, token_ref[1]).astype(BF16)
    values = mm(token_normed, token_ref[2]).astype(BF16)
    row_at = pl.multiple_of(row * tile, 16)
    own = token_normed_ref[pl.ds(row_at, tile), :]
    queries = mm(own, token_ref[0]).astype(BF16)
    gates = sigmoid(mm(own, token_ref[3]).astype(BF16).astype(F32))

    lines = tile * heads
    token_width = queries.shape[1]
    token_head = token_width // heads
    line_of = lax.broadcasted_iota(jnp.int32, (lines, tile), 0) // heads
    repeat = jnp.where(line_of == lax.broadcasted_iota(jnp.int32, (lines, tile), 1), 1.0, 0.0)
    spread = mm(repeat.astype(BF16), queries)
    own_head = lax.rem(lax.broadcasted_iota(jnp.int32, (lines, token_width), 0), heads) == (
        lax.broadcasted_iota(jnp.int32, (lines, token_width), 1) // token_head
    )
    query_lines = jnp.where(own_head, spread, 0.0).astype(BF16)
    scores = mm_nt(query_lines, keys) * (token_head**-0.5)
    arrange(n_chunk - 1)
    scores = scores + bias_full[...].reshape(lines, n_tok)
    query_index = row * tile + lax.broadcasted_iota(jnp.int32, (lines, n_tok), 0) // heads
    key_index = lax.broadcasted_iota(jnp.int32, (lines, n_tok), 1)
    allowed = (token_mask_ref[...] == 1) | (query_index == key_index)
    scores = jnp.where(allowed, scores, NEGATIVE)
    weights = jnp.exp(scores - jnp.max(scores, axis=-1, keepdims=True))
    totals = jnp.sum(weights, axis=-1, keepdims=True)
    weighted = mm(weights.astype(BF16), values) / totals
    weighted = jnp.where(own_head, weighted, 0.0).reshape(tile, heads, token_width)
    token_out_ref[...] = (gates * jnp.sum(weighted, axis=1)).astype(BF16)


def per_device(
    atom_feats,
    atom_bias,
    key_mask,
    atom_token,
    token_mask,
    pair,
    atom_norms,
    w_atom_qkv,
    w_atom_gate,
    w_atom_out,
    w_atom_up,
    w_atom_down,
    w_agg,
    token_norm,
    w_token,
    pair_norms,
    w_pair_up,
    w_pair_down,
    w_bias,
):
    n_row, n_col = lax.axis_size("row"), lax.axis_size("col")
    atom_rows, width = atom_feats.shape
    margin = (KWIN - QWIN) // 2
    tile = pair.shape[0]
    n_tok = token_mask.shape[0]
    heads = w_bias.shape[1]
    c_token = w_agg.shape[1]
    hd = w_token.shape[2]
    n_chunk = tile // PAIR_ROWS
    loaded = (
        atom_bias,
        w_atom_qkv,
        w_atom_gate,
        w_atom_out,
        w_atom_up,
        w_atom_down,
        pair,
        w_pair_up,
        w_pair_down,
        w_agg,
        w_token,
    )
    vmem = pl.BlockSpec(memory_space=pltpu.VMEM)
    dma = pltpu.SemaphoreType.DMA
    return pl.pallas_call(
        functools.partial(kernel, n_row, n_col),
        out_shape=(
            jax.ShapeDtypeStruct((atom_rows, width), BF16),
            jax.ShapeDtypeStruct((tile, hd), BF16),
        ),
        in_specs=[vmem] * 8 + [pl.BlockSpec(memory_space=pl.ANY)] * len(loaded),
        out_specs=(vmem, vmem),
        scratch_shapes=[pltpu.VMEM(x.shape, x.dtype) for x in loaded]
        + [
            pltpu.VMEM((ATOM_BLOCKS, atom_rows, width), BF16),
            pltpu.VMEM((ATOM_BLOCKS, 2, margin, width), BF16),
            pltpu.VMEM((n_row, n_col, atom_rows, width), BF16),
            pltpu.VMEM((n_chunk, n_col, heads, PAIR_ROWS * tile), F32),
            pltpu.VMEM((tile, heads, n_tok), F32),
            pltpu.VMEM((n_tok, c_token), F32),
            pltpu.VMEM((n_tok, 1), F32),
            pltpu.VMEM((n_tok, c_token), BF16),
            dma((len(loaded),)),
            dma((ATOM_BLOCKS, 2)),
            dma((ATOM_BLOCKS, 2)),
            dma((n_col - 1,)),
            dma((n_col - 1,)),
            dma((n_row - 1,)),
            dma((n_row - 1,)),
            dma((n_chunk, n_col - 1)),
            dma((n_chunk, n_col - 1)),
        ],
        compiler_params=pltpu.CompilerParams(
            collective_id=0, has_side_effects=True, vmem_limit_bytes=48 * 1024 * 1024
        ),
    )(
        atom_feats,
        key_mask,
        atom_token.reshape(1, -1),
        token_mask.reshape(1, -1),
        atom_norms,
        token_norm.reshape(1, -1),
        pair_norms,
        w_bias,
        *loaded,
    )


def solution(mesh):
    atoms = ("parts", "row", "col")
    placed = (
        P(atoms, None),
        P(None, atoms, None),
        P(atoms, None),
        P("parts"),
        P("parts"),
        P(("parts", "row"), "col", None),
    ) + (P(),) * 13
    return jax.shard_map(
        per_device,
        mesh=mesh,
        in_specs=placed,
        out_specs=(P(atoms, None), P(("parts", "row"), None)),
        check_vma=False,
    )
```

```python
import functools

import jax
import jax.numpy as jnp
from jax import lax
from jax.experimental import pallas as pl
from jax.experimental.pallas import tpu as pltpu
from jax.sharding import PartitionSpec as P

ATOM_HEADS = 4
ATOM_BLOCKS = 3
QWIN = 32
KWIN = 128
TRANS = 2
PAIR_ROWS = 8
ATOM_STEP = 1024
VMEM_BYTES = 60 * 1024 * 1024
EARLY = 7
LATE = 14

EPSILON = 1e-05
NEGATIVE = -1e30
F32 = jnp.float32
BF16 = jnp.bfloat16
MESH = pl.DeviceIdType.MESH


def layer_norm(inputs, gain):
    average = jnp.mean(inputs, axis=-1, keepdims=True)
    centered = inputs - average
    variance = jnp.mean(centered * centered, axis=-1, keepdims=True)
    return centered * lax.rsqrt(variance + EPSILON) * gain


def sigmoid(value):
    return 0.5 * jnp.tanh(0.5 * value) + 0.5


def mm(left, right):
    return jnp.dot(left, right, preferred_element_type=F32)


def mm_nt(left, right):
    return lax.dot_general(left, right, (((1,), (1,)), ((), ())), preferred_element_type=F32)


def swiglu(normed, w_up, w_down):
    half = w_up.shape[1] // 2
    first = mm(normed, w_up[:, :half])
    second = mm(normed, w_up[:, half:])
    hidden = (first * (jnp.tanh(first) + 1.0) * second).astype(BF16)
    return mm(hidden, w_down)


def split(value):
    high = value.astype(BF16)
    rest = value - high.astype(F32)
    middle = rest.astype(BF16)
    low = (rest - middle.astype(F32)).astype(BF16)
    return high, middle, low


def kernel(
    n_row,
    n_col,
    qkv_any,
    gate_any,
    feats_any,
    atom_norms_any,
    key_mask_any,
    w_bias_any,
    pair_norms_any,
    pair_any,
    pair_up_any,
    pair_down_any,
    bias_any,
    out_any,
    up_any,
    down_any,
    atom_token_any,
    token_mask_any,
    token_norm_any,
    agg_any,
    token_any,
    atom_out_ref,
    token_out_ref,
    qkv_ref,
    gate_ref,
    feats_ref,
    atom_norms_ref,
    key_mask_ref,
    w_bias_ref,
    pair_norms_ref,
    pair_ref,
    pair_up_ref,
    pair_down_ref,
    bias_ref,
    out_ref,
    up_ref,
    down_ref,
    atom_token_ref,
    token_mask_ref,
    token_norm_ref,
    agg_ref,
    token_ref,
    normed_buf,
    rim_buf,
    gathered,
    pair_bias_buf,
    bias_full,
    sums_ref,
    counts_ref,
    token_normed_ref,
    load_sem,
    halo_send,
    halo_recv,
    col_send,
    col_recv,
    row_send,
    row_recv,
    bias_send,
    bias_recv,
):
    row, col = lax.axis_index("row"), lax.axis_index("col")
    rank = row * n_col + col
    n_rank = n_row * n_col
    after, before = lax.rem(rank + 1, n_rank), lax.rem(rank + n_rank - 1, n_rank)
    after_id = {"row": after // n_col, "col": lax.rem(after, n_col)}
    before_id = {"row": before // n_col, "col": lax.rem(before, n_col)}
    col_peers = [lax.rem(col + d, n_col) for d in range(1, n_col)]
    row_peers = [lax.rem(row + d, n_row) for d in range(1, n_row)]

    barrier = pltpu.get_barrier_semaphore()
    for peer in [after_id, before_id] + [{"col": c} for c in col_peers] + [
        {"row": r} for r in row_peers
    ]:
        pl.semaphore_signal(barrier, inc=1, device_id=peer, device_id_type=MESH)

    loads = [
        pltpu.make_async_copy(source, target, load_sem.at[k])
        for k, (source, target) in enumerate(
            (
                (qkv_any, qkv_ref),
                (gate_any, gate_ref),
                (feats_any, feats_ref),
                (atom_norms_any, atom_norms_ref),
                (key_mask_any, key_mask_ref),
                (w_bias_any, w_bias_ref),
                (pair_norms_any, pair_norms_ref),
                (pair_any, pair_ref),
                (pair_up_any, pair_up_ref),
                (pair_down_any, pair_down_ref),
                (bias_any, bias_ref),
                (out_any, out_ref),
                (up_any, up_ref),
                (down_any, down_ref),
                (atom_token_any, atom_token_ref),
                (token_mask_any, token_mask_ref),
                (token_norm_any, token_norm_ref),
                (agg_any, agg_ref),
                (token_any, token_ref),
            )
        )
    ]
    for load in loads:
        load.start()

    atom_rows, width = feats_ref.shape
    head_size = width // ATOM_HEADS
    margin = (KWIN - QWIN) // 2
    n_win = atom_rows // QWIN
    tile = pair_ref.shape[0]
    heads = w_bias_ref.shape[0]
    n_tok = token_mask_ref.shape[1]
    n_chunk = tile // PAIR_ROWS
    flat = PAIR_ROWS * tile

    for load in loads[:EARLY]:
        load.wait()

    slot = lax.broadcasted_iota(jnp.int32, (1, KWIN), 1)
    own_window = (slot >= margin) & (slot < margin + QWIN)
    usable = []
    for win in range(n_win):
        key_index = rank * atom_rows + win * QWIN - margin + slot
        inside = (key_index >= 0) & (key_index < n_rank * atom_rows)
        live = (key_mask_ref[win : win + 1, :] == 1) & inside | own_window
        usable.append(jnp.where(live, 0.0, NEGATIVE))

    lane = lax.broadcasted_iota(jnp.int32, (ATOM_HEADS * QWIN, width), 1)
    line = lax.broadcasted_iota(jnp.int32, (ATOM_HEADS * QWIN, width), 0)
    head_lanes = (lane // head_size) == (line // QWIN)

    w_bias_t = w_bias_ref[...]
    wb_high, wb_middle, wb_low = split(w_bias_t)
    none = jnp.zeros(wb_low.shape, F32)
    wb_stack = jnp.concatenate(
        [
            jnp.concatenate([wb_high.astype(F32), wb_high.astype(F32)], axis=1),
            jnp.concatenate([wb_middle.astype(F32), wb_middle.astype(F32)], axis=1),
            jnp.concatenate([wb_low.astype(F32), none], axis=1),
            jnp.zeros((heads, 2 * width), F32),
        ],
        axis=0,
    ).astype(BF16)

    def bias_copies(chunk):
        return [
            pltpu.make_async_remote_copy(
                src_ref=pair_bias_buf.at[chunk, col],
                dst_ref=pair_bias_buf.at[chunk, col],
                send_sem=bias_send.at[chunk, d],
                recv_sem=bias_recv.at[chunk, d],
                device_id={"col": peer},
                device_id_type=MESH,
            )
            for d, peer in enumerate(col_peers)
        ]

    def pair_chunk(chunk):
        z = pair_ref[pl.ds(chunk * PAIR_ROWS, PAIR_ROWS)].astype(F32).reshape(flat, width)
        for which in range(TRANS):
            normed = layer_norm(z, pair_norms_ref[which : which + 1, :]).astype(BF16)
            z = z + swiglu(normed, pair_up_ref[which], pair_down_ref[which])
        final = layer_norm(z, pair_norms_ref[TRANS : TRANS + 1, :])
        high, middle, low = split(final)
        stacked = mm_nt(wb_stack, jnp.concatenate([high, middle], axis=1))
        total = mm_nt(wb_high, low) + stacked[2 * heads : 3 * heads]
        total = total + stacked[heads : 2 * heads] + stacked[:heads]
        pair_bias_buf[chunk, col] = total
        for copy in bias_copies(chunk):
            copy.start()

    def arrange(chunk):
        for copy in bias_copies(chunk):
            copy.wait()
        for i in range(PAIR_ROWS):
            bias_full[chunk * PAIR_ROWS + i] = jnp.concatenate(
                [pair_bias_buf[chunk, c, :, i * tile : (i + 1) * tile] for c in range(n_col)],
                axis=1,
            )

    def atom_block(block, state):
        normed = layer_norm(state, atom_norms_ref[block, 0:1, :]).astype(BF16)
        normed_buf[block] = normed
        forward = pltpu.make_async_remote_copy(
            src_ref=normed_buf.at[block, pl.ds(atom_rows - margin, margin)],
            dst_ref=rim_buf.at[block, 0],
            send_sem=halo_send.at[block, 0],
            recv_sem=halo_recv.at[block, 0],
            device_id=after_id,
            device_id_type=MESH,
        )
        backward = pltpu.make_async_remote_copy(
            src_ref=normed_buf.at[block, pl.ds(0, margin)],
            dst_ref=rim_buf.at[block, 1],
            send_sem=halo_send.at[block, 1],
            recv_sem=halo_recv.at[block, 1],
            device_id=before_id,
            device_id_type=MESH,
        )
        forward.start()
        backward.start()
        w_qkv = qkv_ref[block]
        qkv = mm(normed, w_qkv)
        gate_rows = sigmoid(mm(normed, gate_ref[block]))
        pair_chunk(block)
        forward.wait()
        backward.wait()
        w_kv = w_qkv[:, width:]
        rim = rim_buf[block].reshape(2 * margin, width)
        rim_kv = mm(rim, w_kv).astype(BF16)
        keyvals = jnp.concatenate(
            [rim_kv[:margin], qkv[:, width:].astype(BF16), rim_kv[margin:]], axis=0
        )
        attended = []
        for win in range(n_win):
            rows = slice(win * QWIN, (win + 1) * QWIN)
            query = jnp.concatenate([qkv[rows, :width]] * ATOM_HEADS, axis=0)
            query = jnp.where(head_lanes, query, 0.0).astype(BF16)
            window = keyvals[win * QWIN : win * QWIN + KWIN]
            bias = bias_ref[:, rows, :].astype(F32).reshape(ATOM_HEADS * QWIN, KWIN)
            scores = mm_nt(query, window[:, :width]) * (head_size**-0.5) + bias
            scores = jnp.where(usable[win] == 0.0, scores, NEGATIVE)
            weights = jnp.exp(scores - jnp.max(scores, axis=-1, keepdims=True))
            totals = jnp.sum(weights, axis=-1, keepdims=True)
            weighted = mm(weights.astype(BF16), window[:, width:]) / totals
            weighted = jnp.where(head_lanes, weighted, 0.0)
            attended.append(
                sum(weighted[h * QWIN : (h + 1) * QWIN] for h in range(ATOM_HEADS))
            )
        mixed = (gate_rows * jnp.concatenate(attended, axis=0)).astype(BF16)
        state = state + mm(mixed, out_ref[block])
        normed_two = layer_norm(state, atom_norms_ref[block, 1:2, :]).astype(BF16)
        return state + swiglu(normed_two, up_ref[block], down_ref[block])

    pl.semaphore_wait(barrier, 2 + n_col - 1 + n_row - 1)
    for load in loads[EARLY:LATE]:
        load.wait()
    for weight in (pair_up_ref, up_ref):
        half = weight.shape[2] // 2
        weight[:, :, :half] = (weight[:, :, :half].astype(F32) * 0.5).astype(BF16)
    state = lax.fori_loop(0, ATOM_BLOCKS, atom_block, feats_ref[...].astype(F32))
    atom_out = state.astype(BF16)
    atom_out_ref[...] = atom_out
    gathered[row, col] = atom_out

    along_col = [
        pltpu.make_async_remote_copy(
            src_ref=gathered.at[row, col],
            dst_ref=gathered.at[row, col],
            send_sem=col_send.at[d],
            recv_sem=col_recv.at[d],
            device_id={"col": peer},
            device_id_type=MESH,
        )
        for d, peer in enumerate(col_peers)
    ]
    for copy in along_col:
        copy.start()
    pair_chunk(ATOM_BLOCKS)
    for copy in along_col:
        copy.wait()
    along_row = [
        pltpu.make_async_remote_copy(
            src_ref=gathered.at[row],
            dst_ref=gathered.at[row],
            send_sem=row_send.at[d],
            recv_sem=row_recv.at[d],
            device_id={"row": peer},
            device_id_type=MESH,
        )
        for d, peer in enumerate(row_peers)
    ]
    for copy in along_row:
        copy.start()

    def rest(chunk, carry):
        pair_chunk(chunk)
        return carry

    lax.fori_loop(ATOM_BLOCKS + 1, n_chunk, rest, 0)

    def place(chunk, carry):
        arrange(chunk)
        return carry

    lax.fori_loop(0, n_chunk - 1, place, 0)
    for load in loads[LATE:]:
        load.wait()
    for copy in along_row:
        copy.wait()

    step_rows = max(1, min(n_row, ATOM_STEP // (n_col * atom_rows)))
    step_atoms = step_rows * n_col * atom_rows
    steps = n_row // step_rows
    w_agg = agg_ref[...]
    token_at = lax.broadcasted_iota(jnp.int32, (n_tok, step_atoms), 0)

    def partial_sums(step):
        atoms = gathered[pl.ds(step * step_rows, step_rows)].reshape(step_atoms, width)
        feat = jnp.maximum(mm(atoms, w_agg), 0.0).astype(BF16)
        tokens = atom_token_ref[:, pl.ds(pl.multiple_of(step * step_atoms, 128), step_atoms)]
        onehot = jnp.where(token_at == tokens, 1.0, 0.0)
        return mm(onehot.astype(BF16), feat), jnp.sum(onehot, axis=1, keepdims=True)

    sums, counts = partial_sums(0)
    if steps > 1:
        sums_ref[...] = sums
        counts_ref[...] = counts

        def more(step, carry):
            extra, number = partial_sums(step)
            sums_ref[...] += extra
            counts_ref[...] += number
            return carry

        lax.fori_loop(1, steps, more, 0)
        sums = sums_ref[...]
        counts = counts_ref[...]
    token_normed = layer_norm(sums / counts, token_norm_ref[...].reshape(1, -1)).astype(BF16)
    token_normed_ref[...] = token_normed
    keys = mm(token_normed, token_ref[1]).astype(BF16)
    values = mm(token_normed, token_ref[2]).astype(BF16)
    row_at = pl.multiple_of(row * tile, 16)
    own = token_normed_ref[pl.ds(row_at, tile), :]
    queries = mm(own, token_ref[0]).astype(BF16)
    gates = sigmoid(mm(own, token_ref[3]).astype(BF16).astype(F32))

    lines = tile * heads
    token_width = queries.shape[1]
    token_head = token_width // heads
    line_of = lax.broadcasted_iota(jnp.int32, (lines, tile), 0) // heads
    repeat = jnp.where(line_of == lax.broadcasted_iota(jnp.int32, (lines, tile), 1), 1.0, 0.0)
    spread = mm(repeat.astype(BF16), queries)
    own_head = lax.rem(lax.broadcasted_iota(jnp.int32, (lines, token_width), 0), heads) == (
        lax.broadcasted_iota(jnp.int32, (lines, token_width), 1) // token_head
    )
    query_lines = jnp.where(own_head, spread, 0.0).astype(BF16)
    scores = mm_nt(query_lines, keys) * (token_head**-0.5)
    arrange(n_chunk - 1)
    scores = scores + bias_full[...].reshape(lines, n_tok)
    query_index = row * tile + lax.broadcasted_iota(jnp.int32, (lines, n_tok), 0) // heads
    key_index = lax.broadcasted_iota(jnp.int32, (lines, n_tok), 1)
    allowed = (token_mask_ref[...] == 1) | (query_index == key_index)
    scores = jnp.where(allowed, scores, NEGATIVE)
    weights = jnp.exp(scores - jnp.max(scores, axis=-1, keepdims=True))
    totals = jnp.sum(weights, axis=-1, keepdims=True)
    weighted = mm(weights.astype(BF16), values) / totals
    weighted = jnp.where(own_head, weighted, 0.0).reshape(tile, heads, token_width)
    token_out_ref[...] = (gates * jnp.sum(weighted, axis=1)).astype(BF16)


def per_device(
    atom_feats,
    atom_bias,
    key_mask,
    atom_token,
    token_mask,
    pair,
    atom_norms,
    w_atom_qkv,
    w_atom_gate,
    w_atom_out,
    w_atom_up,
    w_atom_down,
    w_agg,
    token_norm,
    w_token,
    pair_norms,
    w_pair_up,
    w_pair_down,
    w_bias,
):
    n_row, n_col = lax.axis_size("row"), lax.axis_size("col")
    atom_rows, width = atom_feats.shape
    margin = (KWIN - QWIN) // 2
    tile = pair.shape[0]
    n_tok = token_mask.shape[0]
    heads = w_bias.shape[1]
    c_token = w_agg.shape[1]
    hd = w_token.shape[2]
    n_chunk = tile // PAIR_ROWS
    loaded = (
        w_atom_qkv,
        w_atom_gate,
        atom_feats,
        atom_norms,
        key_mask,
        w_bias.T,
        pair_norms,
        pair,
        w_pair_up,
        w_pair_down,
        atom_bias,
        w_atom_out,
        w_atom_up,
        w_atom_down,
        atom_token.reshape(1, -1),
        token_mask.reshape(1, -1),
        token_norm,
        w_agg,
        w_token,
    )
    vmem = pl.BlockSpec(memory_space=pltpu.VMEM)
    dma = pltpu.SemaphoreType.DMA
    return pl.pallas_call(
        functools.partial(kernel, n_row, n_col),
        out_shape=(
            jax.ShapeDtypeStruct((atom_rows, width), BF16),
            jax.ShapeDtypeStruct((tile, hd), BF16),
        ),
        in_specs=[pl.BlockSpec(memory_space=pltpu.HBM)] * len(loaded),
        out_specs=(vmem, vmem),
        scratch_shapes=[pltpu.VMEM(x.shape, x.dtype) for x in loaded]
        + [
            pltpu.VMEM((ATOM_BLOCKS, atom_rows, width), BF16),
            pltpu.VMEM((ATOM_BLOCKS, 2, margin, width), BF16),
            pltpu.VMEM((n_row, n_col, atom_rows, width), BF16),
            pltpu.VMEM((n_chunk, n_col, heads, PAIR_ROWS * tile), F32),
            pltpu.VMEM((tile, heads, n_tok), F32),
            pltpu.VMEM((n_tok, c_token), F32),
            pltpu.VMEM((n_tok, 1), F32),
            pltpu.VMEM((n_tok, c_token), BF16),
            dma((len(loaded),)),
            dma((ATOM_BLOCKS, 2)),
            dma((ATOM_BLOCKS, 2)),
            dma((n_col - 1,)),
            dma((n_col - 1,)),
            dma((n_row - 1,)),
            dma((n_row - 1,)),
            dma((n_chunk, n_col - 1)),
            dma((n_chunk, n_col - 1)),
        ],
        compiler_params=pltpu.CompilerParams(
            collective_id=0, has_side_effects=True, vmem_limit_bytes=VMEM_BYTES
        ),
    )(*loaded)


def solution(mesh):
    atoms = ("parts", "row", "col")
    placed = (
        P(atoms, None),
        P(None, atoms, None),
        P(atoms, None),
        P("parts"),
        P("parts"),
        P(("parts", "row"), "col", None),
    ) + (P(),) * 13
    return jax.shard_map(
        per_device,
        mesh=mesh,
        in_specs=placed,
        out_specs=(P(atoms, None), P(("parts", "row"), None)),
        check_vma=False,
    )
```

```python
import functools

import jax
import jax.numpy as jnp
from jax import lax
from jax.experimental import pallas as pl
from jax.experimental.pallas import tpu as pltpu
from jax.sharding import PartitionSpec as P

ATOM_HEADS = 4
ATOM_BLOCKS = 3
QWIN = 32
KWIN = 128
TRANS = 2
PAIR_ROWS = 8
ATOM_STEP = 1024
VMEM_BYTES = 60 * 1024 * 1024
EARLY = 7
LATE = 14

EPSILON = 1e-05
NEGATIVE = -1e30
F32 = jnp.float32
BF16 = jnp.bfloat16
MESH = pl.DeviceIdType.MESH


def layer_norm(inputs, gain):
    average = jnp.mean(inputs, axis=-1, keepdims=True)
    centered = inputs - average
    variance = jnp.mean(centered * centered, axis=-1, keepdims=True)
    return centered * lax.rsqrt(variance + EPSILON) * gain


def sigmoid(value):
    return 0.5 * jnp.tanh(0.5 * value) + 0.5


def mm(left, right):
    return jnp.dot(left, right, preferred_element_type=F32)


def mm_nt(left, right):
    return lax.dot_general(left, right, (((1,), (1,)), ((), ())), preferred_element_type=F32)


def swiglu(normed, w_up, w_down):
    half = w_up.shape[1] // 2
    first = mm(normed, w_up[:, :half])
    second = mm(normed, w_up[:, half:])
    hidden = (first * (jnp.tanh(first) + 1.0) * second).astype(BF16)
    return mm(hidden, w_down)


def atoms_at_once(n_row, n_col, atom_rows):
    return max(1, min(n_row, ATOM_STEP // (n_col * atom_rows))) * n_col * atom_rows


def split(value):
    high = value.astype(BF16)
    rest = value - high.astype(F32)
    middle = rest.astype(BF16)
    low = (rest - middle.astype(F32)).astype(BF16)
    return high, middle, low


def kernel(
    n_row,
    n_col,
    qkv_any,
    gate_any,
    feats_any,
    atom_norms_any,
    key_mask_any,
    w_bias_any,
    pair_norms_any,
    pair_any,
    pair_up_any,
    pair_down_any,
    bias_any,
    out_any,
    up_any,
    down_any,
    atom_token_any,
    token_mask_any,
    token_norm_any,
    agg_any,
    token_any,
    atom_out_ref,
    token_out_ref,
    qkv_ref,
    gate_ref,
    feats_ref,
    atom_norms_ref,
    key_mask_ref,
    w_bias_ref,
    pair_norms_ref,
    pair_ref,
    pair_up_ref,
    pair_down_ref,
    bias_ref,
    out_ref,
    up_ref,
    down_ref,
    atom_token_ref,
    token_mask_ref,
    token_norm_ref,
    agg_ref,
    token_ref,
    normed_buf,
    rim_buf,
    gathered,
    pair_bias_buf,
    bias_full,
    sums_ref,
    counts_ref,
    token_normed_ref,
    onehot_ref,
    load_sem,
    halo_send,
    halo_recv,
    col_send,
    col_recv,
    row_send,
    row_recv,
    bias_send,
    bias_recv,
):
    row, col = lax.axis_index("row"), lax.axis_index("col")
    rank = row * n_col + col
    n_rank = n_row * n_col
    after, before = lax.rem(rank + 1, n_rank), lax.rem(rank + n_rank - 1, n_rank)
    after_id = {"row": after // n_col, "col": lax.rem(after, n_col)}
    before_id = {"row": before // n_col, "col": lax.rem(before, n_col)}
    col_peers = [lax.rem(col + d, n_col) for d in range(1, n_col)]
    row_peers = [lax.rem(row + d, n_row) for d in range(1, n_row)]

    barrier = pltpu.get_barrier_semaphore()
    for peer in [after_id, before_id] + [{"col": c} for c in col_peers] + [
        {"row": r} for r in row_peers
    ]:
        pl.semaphore_signal(barrier, inc=1, device_id=peer, device_id_type=MESH)

    loads = [
        pltpu.make_async_copy(source, target, load_sem.at[k])
        for k, (source, target) in enumerate(
            (
                (qkv_any, qkv_ref),
                (gate_any, gate_ref),
                (feats_any, feats_ref),
                (atom_norms_any, atom_norms_ref),
                (key_mask_any, key_mask_ref),
                (w_bias_any, w_bias_ref),
                (pair_norms_any, pair_norms_ref),
                (pair_any, pair_ref),
                (pair_up_any, pair_up_ref),
                (pair_down_any, pair_down_ref),
                (bias_any, bias_ref),
                (out_any, out_ref),
                (up_any, up_ref),
                (down_any, down_ref),
                (atom_token_any, atom_token_ref),
                (token_mask_any, token_mask_ref),
                (token_norm_any, token_norm_ref),
                (agg_any, agg_ref),
                (token_any, token_ref),
            )
        )
    ]
    for load in loads:
        load.start()

    atom_rows, width = feats_ref.shape
    head_size = width // ATOM_HEADS
    margin = (KWIN - QWIN) // 2
    n_win = atom_rows // QWIN
    tile = pair_ref.shape[0]
    heads = w_bias_ref.shape[0]
    n_tok = token_mask_ref.shape[1]
    n_chunk = tile // PAIR_ROWS
    flat = PAIR_ROWS * tile

    for load in loads[:EARLY]:
        load.wait()

    slot = lax.broadcasted_iota(jnp.int32, (1, KWIN), 1)
    own_window = (slot >= margin) & (slot < margin + QWIN)
    usable = []
    for win in range(n_win):
        key_index = rank * atom_rows + win * QWIN - margin + slot
        inside = (key_index >= 0) & (key_index < n_rank * atom_rows)
        live = (key_mask_ref[win : win + 1, :] == 1) & inside | own_window
        usable.append(jnp.where(live, 0.0, NEGATIVE))

    lane = lax.broadcasted_iota(jnp.int32, (ATOM_HEADS * QWIN, width), 1)
    line = lax.broadcasted_iota(jnp.int32, (ATOM_HEADS * QWIN, width), 0)
    head_lanes = (lane // head_size) == (line // QWIN)

    w_bias_t = w_bias_ref[...]
    wb_high, wb_middle, wb_low = split(w_bias_t)
    none = jnp.zeros(wb_low.shape, F32)
    wb_stack = jnp.concatenate(
        [
            jnp.concatenate([wb_high.astype(F32), wb_high.astype(F32)], axis=1),
            jnp.concatenate([wb_middle.astype(F32), wb_middle.astype(F32)], axis=1),
            jnp.concatenate([wb_low.astype(F32), none], axis=1),
            jnp.zeros((heads, 2 * width), F32),
        ],
        axis=0,
    ).astype(BF16)

    def bias_copies(chunk):
        return [
            pltpu.make_async_remote_copy(
                src_ref=pair_bias_buf.at[chunk, col],
                dst_ref=pair_bias_buf.at[chunk, col],
                send_sem=bias_send.at[chunk, d],
                recv_sem=bias_recv.at[chunk, d],
                device_id={"col": peer},
                device_id_type=MESH,
            )
            for d, peer in enumerate(col_peers)
        ]

    def pair_chunk(chunk):
        z = pair_ref[pl.ds(chunk * PAIR_ROWS, PAIR_ROWS)].astype(F32).reshape(flat, width)
        for which in range(TRANS):
            normed = layer_norm(z, pair_norms_ref[which : which + 1, :]).astype(BF16)
            z = z + swiglu(normed, pair_up_ref[which], pair_down_ref[which])
        final = layer_norm(z, pair_norms_ref[TRANS : TRANS + 1, :])
        high, middle, low = split(final)
        stacked = mm_nt(wb_stack, jnp.concatenate([high, middle], axis=1))
        total = mm_nt(wb_high, low) + stacked[2 * heads : 3 * heads]
        total = total + stacked[heads : 2 * heads] + stacked[:heads]
        pair_bias_buf[chunk, col] = total
        for copy in bias_copies(chunk):
            copy.start()

    def arrange(chunk):
        for copy in bias_copies(chunk):
            copy.wait()
        for i in range(PAIR_ROWS):
            bias_full[chunk * PAIR_ROWS + i] = jnp.concatenate(
                [pair_bias_buf[chunk, c, :, i * tile : (i + 1) * tile] for c in range(n_col)],
                axis=1,
            )

    def atom_block(block, state):
        normed = layer_norm(state, atom_norms_ref[block, 0:1, :]).astype(BF16)
        normed_buf[block] = normed
        forward = pltpu.make_async_remote_copy(
            src_ref=normed_buf.at[block, pl.ds(atom_rows - margin, margin)],
            dst_ref=rim_buf.at[block, 0],
            send_sem=halo_send.at[block, 0],
            recv_sem=halo_recv.at[block, 0],
            device_id=after_id,
            device_id_type=MESH,
        )
        backward = pltpu.make_async_remote_copy(
            src_ref=normed_buf.at[block, pl.ds(0, margin)],
            dst_ref=rim_buf.at[block, 1],
            send_sem=halo_send.at[block, 1],
            recv_sem=halo_recv.at[block, 1],
            device_id=before_id,
            device_id_type=MESH,
        )
        forward.start()
        backward.start()

        @pl.when(block == 0)
        def _():
            for load in loads[EARLY:LATE]:
                load.wait()
            for weight in (pair_up_ref, up_ref):
                half = weight.shape[2] // 2
                weight[:, :, :half] = (weight[:, :, :half].astype(F32) * 0.5).astype(BF16)

        w_qkv = qkv_ref[block]
        qkv = mm(normed, w_qkv)
        gate_rows = sigmoid(mm(normed, gate_ref[block]))
        pair_chunk(block)
        forward.wait()
        backward.wait()
        w_kv = w_qkv[:, width:]
        rim = rim_buf[block].reshape(2 * margin, width)
        rim_kv = mm(rim, w_kv).astype(BF16)
        keyvals = jnp.concatenate(
            [rim_kv[:margin], qkv[:, width:].astype(BF16), rim_kv[margin:]], axis=0
        )
        attended = []
        for win in range(n_win):
            rows = slice(win * QWIN, (win + 1) * QWIN)
            query = jnp.concatenate([qkv[rows, :width]] * ATOM_HEADS, axis=0)
            query = jnp.where(head_lanes, query, 0.0).astype(BF16)
            window = keyvals[win * QWIN : win * QWIN + KWIN]
            bias = bias_ref[:, rows, :].astype(F32).reshape(ATOM_HEADS * QWIN, KWIN)
            scores = mm_nt(query, window[:, :width]) * (head_size**-0.5) + bias
            scores = jnp.where(usable[win] == 0.0, scores, NEGATIVE)
            weights = jnp.exp(scores - jnp.max(scores, axis=-1, keepdims=True))
            totals = jnp.sum(weights, axis=-1, keepdims=True)
            weighted = mm(weights.astype(BF16), window[:, width:]) * (1.0 / totals)
            weighted = jnp.where(head_lanes, weighted, 0.0)
            attended.append(
                sum(weighted[h * QWIN : (h + 1) * QWIN] for h in range(ATOM_HEADS))
            )
        mixed = (gate_rows * jnp.concatenate(attended, axis=0)).astype(BF16)
        state = state + mm(mixed, out_ref[block])
        normed_two = layer_norm(state, atom_norms_ref[block, 1:2, :]).astype(BF16)
        return state + swiglu(normed_two, up_ref[block], down_ref[block])

    pl.semaphore_wait(barrier, 2 + n_col - 1 + n_row - 1)
    state = lax.fori_loop(0, ATOM_BLOCKS, atom_block, feats_ref[...].astype(F32))
    atom_out = state.astype(BF16)
    atom_out_ref[...] = atom_out
    gathered[row, col] = atom_out

    along_col = [
        pltpu.make_async_remote_copy(
            src_ref=gathered.at[row, col],
            dst_ref=gathered.at[row, col],
            send_sem=col_send.at[d],
            recv_sem=col_recv.at[d],
            device_id={"col": peer},
            device_id_type=MESH,
        )
        for d, peer in enumerate(col_peers)
    ]
    for copy in along_col:
        copy.start()
    pair_chunk(ATOM_BLOCKS)
    for copy in along_col:
        copy.wait()
    along_row = [
        pltpu.make_async_remote_copy(
            src_ref=gathered.at[row],
            dst_ref=gathered.at[row],
            send_sem=row_send.at[d],
            recv_sem=row_recv.at[d],
            device_id={"row": peer},
            device_id_type=MESH,
        )
        for d, peer in enumerate(row_peers)
    ]
    for copy in along_row:
        copy.start()

    def rest(chunk, carry):
        pair_chunk(chunk)
        return carry

    lax.fori_loop(ATOM_BLOCKS + 1, n_chunk, rest, 0)

    def place(chunk, carry):
        arrange(chunk)
        return carry

    lax.fori_loop(0, n_chunk - 1, place, 0)
    for load in loads[LATE:]:
        load.wait()

    step_atoms = atoms_at_once(n_row, n_col, atom_rows)
    step_rows = step_atoms // (n_col * atom_rows)
    steps = n_row // step_rows
    w_agg = agg_ref[...]
    token_at = lax.broadcasted_iota(jnp.int32, (n_tok, step_atoms), 0)

    def members(step):
        tokens = atom_token_ref[:, pl.ds(pl.multiple_of(step * step_atoms, 128), step_atoms)]
        onehot = jnp.where(token_at == tokens, 1.0, 0.0)
        return onehot.astype(BF16), jnp.sum(onehot, axis=1, keepdims=True)

    def partial_sums(step, onehot):
        atoms = gathered[pl.ds(step * step_rows, step_rows)].reshape(step_atoms, width)
        feat = jnp.maximum(mm(atoms, w_agg), 0.0).astype(BF16)
        return mm(onehot, feat)

    onehot, counts = members(0)
    onehot_ref[...] = onehot
    for copy in along_row:
        copy.wait()
    sums = partial_sums(0, onehot_ref[...])
    if steps > 1:
        sums_ref[...] = sums
        counts_ref[...] = counts

        def more(step, carry):
            onehot, number = members(step)
            sums_ref[...] += partial_sums(step, onehot)
            counts_ref[...] += number
            return carry

        lax.fori_loop(1, steps, more, 0)
        sums = sums_ref[...]
        counts = counts_ref[...]
    token_normed = layer_norm(sums * (1.0 / counts), token_norm_ref[...].reshape(1, -1)).astype(BF16)
    token_normed_ref[...] = token_normed
    keys = mm(token_normed, token_ref[1]).astype(BF16)
    values = mm(token_normed, token_ref[2]).astype(BF16)
    row_at = pl.multiple_of(row * tile, 16)
    own = token_normed_ref[pl.ds(row_at, tile), :]
    queries = mm(own, token_ref[0]).astype(BF16)
    gates = sigmoid(mm(own, token_ref[3]).astype(BF16).astype(F32))

    lines = tile * heads
    token_width = queries.shape[1]
    token_head = token_width // heads
    line_of = lax.broadcasted_iota(jnp.int32, (lines, tile), 0) // heads
    repeat = jnp.where(line_of == lax.broadcasted_iota(jnp.int32, (lines, tile), 1), 1.0, 0.0)
    spread = mm(repeat.astype(BF16), queries)
    own_head = lax.rem(lax.broadcasted_iota(jnp.int32, (lines, token_width), 0), heads) == (
        lax.broadcasted_iota(jnp.int32, (lines, token_width), 1) // token_head
    )
    query_lines = jnp.where(own_head, spread, 0.0).astype(BF16)
    scores = mm_nt(query_lines, keys) * (token_head**-0.5)
    arrange(n_chunk - 1)
    scores = scores + bias_full[...].reshape(lines, n_tok)
    query_index = row * tile + lax.broadcasted_iota(jnp.int32, (lines, n_tok), 0) // heads
    key_index = lax.broadcasted_iota(jnp.int32, (lines, n_tok), 1)
    allowed = (token_mask_ref[...] == 1) | (query_index == key_index)
    scores = jnp.where(allowed, scores, NEGATIVE)
    weights = jnp.exp(scores - jnp.max(scores, axis=-1, keepdims=True))
    totals = jnp.sum(weights, axis=-1, keepdims=True)
    weighted = mm(weights.astype(BF16), values) * (1.0 / totals)
    weighted = jnp.where(own_head, weighted, 0.0).reshape(tile, heads, token_width)
    token_out_ref[...] = (gates * jnp.sum(weighted, axis=1)).astype(BF16)


def per_device(
    atom_feats,
    atom_bias,
    key_mask,
    atom_token,
    token_mask,
    pair,
    atom_norms,
    w_atom_qkv,
    w_atom_gate,
    w_atom_out,
    w_atom_up,
    w_atom_down,
    w_agg,
    token_norm,
    w_token,
    pair_norms,
    w_pair_up,
    w_pair_down,
    w_bias,
):
    n_row, n_col = lax.axis_size("row"), lax.axis_size("col")
    atom_rows, width = atom_feats.shape
    margin = (KWIN - QWIN) // 2
    tile = pair.shape[0]
    n_tok = token_mask.shape[0]
    heads = w_bias.shape[1]
    c_token = w_agg.shape[1]
    hd = w_token.shape[2]
    n_chunk = tile // PAIR_ROWS
    loaded = (
        w_atom_qkv,
        w_atom_gate,
        atom_feats,
        atom_norms,
        key_mask,
        w_bias.T,
        pair_norms,
        pair,
        w_pair_up,
        w_pair_down,
        atom_bias,
        w_atom_out,
        w_atom_up,
        w_atom_down,
        atom_token.reshape(1, -1),
        token_mask.reshape(1, -1),
        token_norm,
        w_agg,
        w_token,
    )
    vmem = pl.BlockSpec(memory_space=pltpu.VMEM)
    dma = pltpu.SemaphoreType.DMA
    return pl.pallas_call(
        functools.partial(kernel, n_row, n_col),
        out_shape=(
            jax.ShapeDtypeStruct((atom_rows, width), BF16),
            jax.ShapeDtypeStruct((tile, hd), BF16),
        ),
        in_specs=[pl.BlockSpec(memory_space=pltpu.HBM)] * len(loaded),
        out_specs=(vmem, vmem),
        scratch_shapes=[pltpu.VMEM(x.shape, x.dtype) for x in loaded]
        + [
            pltpu.VMEM((ATOM_BLOCKS, atom_rows, width), BF16),
            pltpu.VMEM((ATOM_BLOCKS, 2, margin, width), BF16),
            pltpu.VMEM((n_row, n_col, atom_rows, width), BF16),
            pltpu.VMEM((n_chunk, n_col, heads, PAIR_ROWS * tile), F32),
            pltpu.VMEM((tile, heads, n_tok), F32),
            pltpu.VMEM((n_tok, c_token), F32),
            pltpu.VMEM((n_tok, 1), F32),
            pltpu.VMEM((n_tok, c_token), BF16),
            pltpu.VMEM((n_tok, atoms_at_once(n_row, n_col, atom_rows)), BF16),
            dma((len(loaded),)),
            dma((ATOM_BLOCKS, 2)),
            dma((ATOM_BLOCKS, 2)),
            dma((n_col - 1,)),
            dma((n_col - 1,)),
            dma((n_row - 1,)),
            dma((n_row - 1,)),
            dma((n_chunk, n_col - 1)),
            dma((n_chunk, n_col - 1)),
        ],
        compiler_params=pltpu.CompilerParams(
            collective_id=0, has_side_effects=True, vmem_limit_bytes=VMEM_BYTES
        ),
    )(*loaded)


def solution(mesh):
    atoms = ("parts", "row", "col")
    placed = (
        P(atoms, None),
        P(None, atoms, None),
        P(atoms, None),
        P("parts"),
        P("parts"),
        P(("parts", "row"), "col", None),
    ) + (P(),) * 13
    return jax.shard_map(
        per_device,
        mesh=mesh,
        in_specs=placed,
        out_specs=(P(atoms, None), P(("parts", "row"), None)),
        check_vma=False,
    )
```
